32 devices in a mesh: ta: 4 (over y, x), sa: 8 (over z, core).
Axes of the slice: x: 2, y: 2, z: 4, core: 2. Of those that a mesh axis runs over, the one named last changes fastest.
Arguments:
- perambulator: bfloat16 [2, 4, 8, 384, 384], P(None, None, 'sa', 'ta'), may hold values from -6 to 6
- meson_ops: bfloat16 [2, 8, 4, 384, 384], P(None, None, 'ta'), may hold values from -0.21875 to 0.21875
- diagram_lists: int32 [4, 64, 2], P('ta', 'sa'), may hold values from 0 to 63, as said below
Outputs:
- correlators: float32 [2, 4, 8, 384, 384], P(None, 'ta', 'sa')
The draws below stay inside these ranges and needn't reach their ends.
Inputs may be any that keep to these rules, and one draw needn't show every extreme that they name: `diagram_lists`: every id lies in 0 to 63. Among the 16 ids of one owner's list, no spin pair (id // 8) occurs more than 2 times, and at least one spin pair occurs exactly 2 times; several may.
All inputs are finite; a program needn't handle non-finite values.
Results may differ from the reference program's by a relative error of at most 0.004.
Values may be sent and summed in bfloat16 or wider, within the bound.
A program may use at most 128 MiB of HBM per device.

```python
import jax
import jax.numpy as jnp
from jax import lax

NEV = 384
OPS = 8
PAIRS = 8
CAP = 2
TS = 4
SPIN = 8
OWNERS = 8


def owner_list(key):
    key_hot, key_perm, key_order, key_ops = jax.random.split(key, 4)
    hot_spin = jax.random.randint(key_hot, (), 0, SPIN)
    shuffled = jax.random.permutation(key_perm, (SPIN - 1) * CAP)
    others = shuffled[:2 * PAIRS - CAP] // CAP
    others = others + (others >= hot_spin).astype(jnp.int32)
    spin_ids = jnp.concatenate([jnp.full((CAP,), hot_spin, jnp.int32), others.astype(jnp.int32)])
    order = jax.random.permutation(key_order, 2 * PAIRS)
    spin_ids = spin_ids[order]
    op_ids = jax.random.randint(key_ops, (2 * PAIRS,), 0, OPS)
    return (spin_ids * OPS + op_ids).astype(jnp.int32).reshape(PAIRS, 2)


def draw_diagram_lists(key, part):
    keys = jax.random.split(jax.random.fold_in(key, 7), TS * OWNERS)
    lists = jax.vmap(owner_list)(keys)
    return lists.reshape(TS, OWNERS * PAIRS, 2)


def level_of(stream_key, dims, cuts, smallest, largest):
    def one(axis_at, parts):
        draws = jax.random.uniform(jax.random.fold_in(jax.random.fold_in(stream_key, 6), axis_at), (parts,), jnp.float32, smallest / len(cuts), largest / len(cuts))
        return jnp.repeat(jnp.exp(draws), dims[axis_at] // parts).reshape((-1,) + (1,) * (len(dims) - axis_at - 1))

    factor_of = one(*cuts[0])
    for cut in cuts[1:]:
        factor_of = factor_of * one(*cut)
    return factor_of


def scatter_about(rng, dims, deviation, reach, shards=(), dtype=jnp.bfloat16):
    drawn = deviation * jax.random.normal(rng, dims, jnp.float32)
    if shards:
        drawn = drawn * level_of(rng, dims, shards, -0.22, 0.18)
    return jnp.clip(drawn, -reach, reach).astype(dtype)


def setup_inputs(seed: int = 0) -> dict:
    arg_keys = jax.random.split(jax.random.key(seed), 4)
    perambulator = scatter_about(arg_keys[0], (2, TS, SPIN, NEV, NEV), 1.0, 6.0, ((2, 8), (3, 4)))
    meson_ops = scatter_about(arg_keys[1], (2, OPS, TS, NEV, NEV), (2 * NEV) ** -0.5, 0.21875, ((2, 4),))
    diagram_lists = draw_diagram_lists(jax.random.fold_in(arg_keys[3], 71), 0)
    return dict(perambulator=perambulator, meson_ops=meson_ops, diagram_lists=diagram_lists)


def one_time(inputs):
    peram_time, ops_time, lists_time = inputs
    op_real = ops_time[0].astype(jnp.float32)
    op_imag = ops_time[1].astype(jnp.float32)
    pr_real = peram_time[0].astype(jnp.float32)
    pr_imag = peram_time[1].astype(jnp.float32)
    block_real = jnp.einsum('oik,sjk->soij', op_real, pr_real) - jnp.einsum('oik,sjk->soij', op_imag, pr_imag)
    block_imag = jnp.einsum('oik,sjk->soij', op_real, pr_imag) + jnp.einsum('oik,sjk->soij', op_imag, pr_real)
    blocks = jnp.stack([block_real, block_imag]).astype(jnp.bfloat16)
    blocks = blocks.reshape(2, SPIN * OPS, NEV, NEV)
    block_ids = lists_time.reshape(OWNERS, PAIRS, 2).astype(jnp.int32)
    first = blocks[:, block_ids[:, :, 0]].astype(jnp.float32)
    second = blocks[:, block_ids[:, :, 1]].astype(jnp.float32)
    real_sum = jnp.einsum('wpik,wpkj->wij', first[0], second[0]) - jnp.einsum('wpik,wpkj->wij', first[1], second[1])
    imag_sum = jnp.einsum('wpik,wpkj->wij', first[0], second[1]) + jnp.einsum('wpik,wpkj->wij', first[1], second[0])
    normalizer = 1.0 / jnp.sqrt(jnp.float32(2 * NEV * PAIRS))
    return jnp.stack([real_sum, imag_sum]) * normalizer

def reference(perambulator, meson_ops, diagram_lists):
    results = lax.map(one_time, (jnp.moveaxis(perambulator, 1, 0), jnp.moveaxis(meson_ops, 2, 0), diagram_lists))
    return jnp.moveaxis(results, 0, 1)
```

```python
import functools

import jax
import jax.numpy as jnp
from jax import lax
from jax.experimental import pallas as pl
from jax.experimental.pallas import tpu as pltpu
from jax.sharding import PartitionSpec as P

CORES = 2
CAP = 2
MESH = pl.DeviceIdType.MESH


def kernel(
    ta, sa, op_table, pair_slots, peram, ops, out, held, ops_here, factors, total,
    send_sem, recv_sem, local_sem,
):
    chips = sa // CORES
    half = chips // 2
    a = lax.axis_index("ta")
    me = lax.axis_index("sa")
    z, core = me // CORES, lax.rem(me, CORES)
    eig = ops.shape[-1]

    def spin_at(offset, parity):
        return lax.rem(z + offset + chips, chips) * CORES + parity

    up = (a, spin_at(1, core))
    down = (a, spin_at(-1, core))
    sibling = (a, z * CORES + 1 - core)
    plane = [(lax.rem(a + j, ta), me) for j in range(1, ta)]

    load_ops = pltpu.make_async_copy(ops.at[:, :, 0], ops_here, local_sem.at[0])
    load_ops.start()
    load_own = pltpu.make_async_copy(peram.at[:, a, 0], held.at[me, 0], local_sem.at[1])
    load_own.start()

    barrier = pltpu.get_barrier_semaphore()
    peers = [*plane, up, down, sibling]
    for peer in peers:
        pl.semaphore_signal(barrier, inc=1, device_id=peer, device_id_type=MESH)
    pl.semaphore_wait(barrier, len(peers))

    sent = []

    def send(src, spin, slot, peer):
        copy = pltpu.make_async_remote_copy(
            src_ref=src,
            dst_ref=held.at[spin, slot],
            send_sem=send_sem.at[len(sent)],
            recv_sem=recv_sem.at[spin, slot],
            device_id=peer,
            device_id_type=MESH,
        )
        copy.start()
        sent.append(copy)

    def arrived(spin, slot):
        pltpu.make_async_remote_copy(
            src_ref=held.at[spin, slot],
            dst_ref=held.at[spin, slot],
            send_sem=send_sem.at[0],
            recv_sem=recv_sem.at[spin, slot],
            device_id=sibling,
            device_id_type=MESH,
        ).wait_recv()

    def hops_up(i):
        return half if i < ta // 2 else chips - 1 - half

    def hops_down(i):
        return chips - 1 - hops_up(i)

    def factor(spin):
        at = [lax.rem(q - a + ta, ta) for q in range(ta)]
        real = jnp.concatenate([held[spin, i, 0] for i in at], axis=0)
        imag = jnp.concatenate([held[spin, i, 1] for i in at], axis=0)
        right = jnp.concatenate(
            [jnp.concatenate([real, -imag], axis=1), jnp.concatenate([imag, real], axis=1)], axis=0
        )
        lefts = []
        for c in range(CAP):
            op = op_table[spin * CAP + c]
            lefts.append(jnp.concatenate([ops_here[0, op], ops_here[1, op]], axis=1))
        both = lax.dot_general(
            jnp.concatenate(lefts, axis=0), right, (((1,), (1,)), ((), ())),
            preferred_element_type=jnp.float32,
        )
        for c in range(CAP):
            factors[spin * CAP + c] = both[c * eig:(c + 1) * eig].astype(jnp.bfloat16)

    own = peram.at[:, a, 0]
    for peer in (up, down, sibling):
        send(own, me, 0, peer)
    for j in range(1, ta):
        send(peram.at[:, plane[j - 1][0], 0], me, ta - j, plane[j - 1])
    for i in range(ta - 1, 0, -1):
        arrived(me, i)
        for peer in (up, down, sibling):
            send(held.at[me, i], me, i, peer)

    load_ops.wait()
    load_own.wait()
    other = z * CORES + 1 - core
    for i in range(ta):
        arrived(other, i)

    def own_chip(n, carry):
        factor(z * CORES + n)
        return carry

    lax.fori_loop(0, CORES, own_chip, 0)

    for h in range(1, half + 1):
        below, above = spin_at(-h, core), spin_at(h, core)
        order = [0, *range(ta - 1, 0, -1)]
        for i in order:
            if hops_up(i) >= h:
                arrived(below, i)
                if hops_up(i) > h:
                    send(held.at[below, i], below, i, up)
                send(held.at[below, i], below, i, sibling)
            if hops_down(i) >= h:
                arrived(above, i)
                if hops_down(i) > h:
                    send(held.at[above, i], above, i, down)
                send(held.at[above, i], above, i, sibling)
        count = 2 if 2 * h < chips else 1

        def ready(n, carry):
            factor(spin_at(jnp.where(n == 0, -h, h), core))
            return carry

        lax.fori_loop(0, count, ready, 0)
        for offset in (-h, h)[:count]:
            for i in range(ta):
                arrived(spin_at(offset, 1 - core), i)

        def siblings(n, carry):
            factor(spin_at(jnp.where(n == 0, -h, h), 1 - core))
            return carry

        lax.fori_loop(0, count, siblings, 0)

    total[...] = jnp.zeros_like(total)

    def pair(p, carry):
        left = factors[pair_slots[2 * p]]
        second = factors[pair_slots[2 * p + 1]]
        real, imag = second[:, :eig], second[:, eig:]
        right = jnp.concatenate([second, jnp.concatenate([-imag, real], axis=1)], axis=0)
        total[...] += jnp.dot(left, right, preferred_element_type=jnp.float32)
        return carry

    pairs = pair_slots.shape[0] // 2
    lax.fori_loop(0, pairs, pair, 0)
    normalizer = 1.0 / jnp.sqrt(jnp.float32(2 * eig * pairs))
    out[0] = total[:, :eig] * normalizer
    out[1] = total[:, eig:] * normalizer
    for copy in sent:
        copy.wait_send()


def body(ta, sa, perambulator, meson_ops, diagram_lists):
    ops_count, eig = meson_ops.shape[1], meson_ops.shape[-1]
    rows = perambulator.shape[3]
    ids = diagram_lists[0].reshape(-1)
    spins = ids // ops_count
    ahead = jnp.arange(ids.shape[0])[:, None] > jnp.arange(ids.shape[0])[None, :]
    rank = jnp.sum((spins[:, None] == spins[None, :]) & ahead, axis=1, dtype=jnp.int32)
    slots = spins * CAP + rank
    here = slots[None, :] == jnp.arange(sa * CAP)[:, None]
    op_table = jnp.sum(jnp.where(here, (ids % ops_count)[None, :], 0), axis=1, dtype=jnp.int32)
    chips = sa // CORES
    sends = (ta - 1) + ta * (chips - 1 + chips)
    flops = 2 * (2 * eig) ** 2 * eig * (sa * CAP + ids.shape[0] // 2)
    result = pl.pallas_call(
        functools.partial(kernel, ta, sa),
        out_shape=jax.ShapeDtypeStruct((2, eig, eig), jnp.float32),
        in_specs=[
            pl.BlockSpec(memory_space=pltpu.SMEM),
            pl.BlockSpec(memory_space=pltpu.SMEM),
            pl.BlockSpec(memory_space=pl.ANY),
            pl.BlockSpec(memory_space=pl.ANY),
        ],
        out_specs=pl.BlockSpec(memory_space=pltpu.VMEM),
        scratch_shapes=[
            pltpu.VMEM((sa, ta, 2, rows, eig), jnp.bfloat16),
            pltpu.VMEM((2, ops_count, eig, eig), jnp.bfloat16),
            pltpu.VMEM((sa * CAP, eig, 2 * eig), jnp.bfloat16),
            pltpu.VMEM((eig, 2 * eig), jnp.float32),
            pltpu.SemaphoreType.DMA((sends,)),
            pltpu.SemaphoreType.DMA((sa, ta)),
            pltpu.SemaphoreType.DMA((2,)),
        ],
        compiler_params=pltpu.CompilerParams(
            collective_id=0, has_side_effects=True, vmem_limit_bytes=56 * 2**20
        ),
        cost_estimate=pl.CostEstimate(
            flops=flops, bytes_accessed=4 * meson_ops.size, transcendentals=0
        ),
    )(op_table, slots, perambulator, meson_ops)
    return result[:, None, None]


def solution(mesh):
    in_specs = (
        P(None, None, "sa", "ta", None),
        P(None, None, "ta", None, None),
        P("ta", "sa", None),
    )
    out_specs = P(None, "ta", "sa", None, None)
    return jax.shard_map(
        functools.partial(body, mesh.shape["ta"], mesh.shape["sa"]),
        mesh=mesh, in_specs=in_specs, out_specs=out_specs, check_vma=False,
    )
```

```python
import functools

import jax
import jax.numpy as jnp
from jax import lax
from jax.experimental import pallas as pl
from jax.experimental.pallas import tpu as pltpu
from jax.sharding import PartitionSpec as P

CORES = 2
CAP = 2
MESH = pl.DeviceIdType.MESH


def kernel(
    ta, sa, op_table, pair_slots, peram, ops, out, held, ops_here, factors,
    send_sem, recv_sem, local_sem,
):
    chips = sa // CORES
    half = chips // 2
    a = lax.axis_index("ta")
    me = lax.axis_index("sa")
    z, core = me // CORES, lax.rem(me, CORES)
    eig = ops.shape[-1]

    def spin_at(offset, parity):
        return lax.rem(z + offset + chips, chips) * CORES + parity

    up = (a, spin_at(1, core))
    down = (a, spin_at(-1, core))
    sibling = (a, z * CORES + 1 - core)
    plane = [(lax.rem(a + j, ta), me) for j in range(1, ta)]

    load_ops = pltpu.make_async_copy(ops.at[:, :, 0], ops_here, local_sem.at[0])
    load_ops.start()
    load_own = pltpu.make_async_copy(peram.at[:, a, 0], held.at[me, 0], local_sem.at[1])
    load_own.start()

    barrier = pltpu.get_barrier_semaphore()
    peers = [*plane, up, down, sibling]
    for peer in peers:
        pl.semaphore_signal(barrier, inc=1, device_id=peer, device_id_type=MESH)
    pl.semaphore_wait(barrier, len(peers))

    sent = []

    def send(src, spin, slot, peer):
        copy = pltpu.make_async_remote_copy(
            src_ref=src,
            dst_ref=held.at[spin, slot],
            send_sem=send_sem.at[len(sent)],
            recv_sem=recv_sem.at[spin, slot],
            device_id=peer,
            device_id_type=MESH,
        )
        copy.start()
        sent.append(copy)

    def arrived(spin, slot):
        pltpu.make_async_remote_copy(
            src_ref=held.at[spin, slot],
            dst_ref=held.at[spin, slot],
            send_sem=send_sem.at[0],
            recv_sem=recv_sem.at[spin, slot],
            device_id=sibling,
            device_id_type=MESH,
        ).wait_recv()

    def hops_up(i):
        return half if i < ta // 2 else chips - 1 - half

    def hops_down(i):
        return chips - 1 - hops_up(i)

    def factor(spin):
        at = [lax.rem(q - a + ta, ta) for q in range(ta)]
        real = jnp.concatenate([held[spin, i, 0] for i in at], axis=0)
        imag = jnp.concatenate([held[spin, i, 1] for i in at], axis=0)
        right = jnp.concatenate(
            [jnp.concatenate([real, -imag], axis=1), jnp.concatenate([imag, real], axis=1)], axis=0
        )
        lefts = []
        for c in range(CAP):
            op = op_table[spin * CAP + c]
            lefts.append(jnp.concatenate([ops_here[0, op], ops_here[1, op]], axis=1))
        both = lax.dot_general(
            jnp.concatenate(lefts, axis=0), right, (((1,), (1,)), ((), ())),
            preferred_element_type=jnp.float32,
        )
        for c in range(CAP):
            factors[spin * CAP + c] = both[c * eig:(c + 1) * eig].astype(jnp.bfloat16)

    own = peram.at[:, a, 0]
    for peer in (up, down, sibling):
        send(own, me, 0, peer)
    for j in range(1, ta):
        send(peram.at[:, plane[j - 1][0], 0], me, ta - j, plane[j - 1])
    for i in range(ta - 1, 0, -1):
        arrived(me, i)
        for peer in (up, down, sibling):
            send(held.at[me, i], me, i, peer)

    out[...] = jnp.zeros_like(out)
    load_ops.wait()
    load_own.wait()
    other = z * CORES + 1 - core
    for i in range(ta):
        arrived(other, i)

    def own_chip(n, carry):
        factor(z * CORES + n)
        return carry

    lax.fori_loop(0, CORES, own_chip, 0)

    for h in range(1, half + 1):
        below, above = spin_at(-h, core), spin_at(h, core)
        order = [0, *range(ta - 1, 0, -1)]
        for i in order:
            if hops_up(i) >= h:
                arrived(below, i)
                if hops_up(i) > h:
                    send(held.at[below, i], below, i, up)
                send(held.at[below, i], below, i, sibling)
            if hops_down(i) >= h:
                arrived(above, i)
                if hops_down(i) > h:
                    send(held.at[above, i], above, i, down)
                send(held.at[above, i], above, i, sibling)
        count = 2 if 2 * h < chips else 1

        def ready(n, carry):
            factor(spin_at(jnp.where(n == 0, -h, h), core))
            return carry

        lax.fori_loop(0, count, ready, 0)
        for offset in (-h, h)[:count]:
            for i in range(ta):
                arrived(spin_at(offset, 1 - core), i)

        def siblings(n, carry):
            factor(spin_at(jnp.where(n == 0, -h, h), 1 - core))
            return carry

        lax.fori_loop(0, count, siblings, 0)

    def pair(p, carry):
        left = factors[pair_slots[2 * p]]
        second = factors[pair_slots[2 * p + 1]]
        real, imag = second[:, :eig], second[:, eig:]
        right = jnp.concatenate([second, jnp.concatenate([-imag, real], axis=1)], axis=0)
        both = jnp.dot(left, right, preferred_element_type=jnp.float32)
        out[0] += both[:, :eig]
        out[1] += both[:, eig:]
        return carry

    pairs = pair_slots.shape[0] // 2
    lax.fori_loop(0, pairs, pair, 0, unroll=2)
    for copy in sent:
        copy.wait_send()


def body(ta, sa, perambulator, meson_ops, diagram_lists):
    ops_count, eig = meson_ops.shape[1], meson_ops.shape[-1]
    rows = perambulator.shape[3]
    ids = diagram_lists[0].reshape(-1)
    spins = ids // ops_count
    ahead = jnp.arange(ids.shape[0])[:, None] > jnp.arange(ids.shape[0])[None, :]
    rank = jnp.sum((spins[:, None] == spins[None, :]) & ahead, axis=1, dtype=jnp.int32)
    slots = spins * CAP + rank
    here = slots[None, :] == jnp.arange(sa * CAP)[:, None]
    op_table = jnp.sum(jnp.where(here, (ids % ops_count)[None, :], 0), axis=1, dtype=jnp.int32)
    chips = sa // CORES
    sends = (ta - 1) + ta * (chips - 1 + chips)
    flops = 2 * (2 * eig) ** 2 * eig * (sa * CAP + ids.shape[0] // 2)
    result = pl.pallas_call(
        functools.partial(kernel, ta, sa),
        out_shape=jax.ShapeDtypeStruct((2, eig, eig), jnp.float32),
        in_specs=[
            pl.BlockSpec(memory_space=pltpu.SMEM),
            pl.BlockSpec(memory_space=pltpu.SMEM),
            pl.BlockSpec(memory_space=pl.ANY),
            pl.BlockSpec(memory_space=pl.ANY),
        ],
        out_specs=pl.BlockSpec(memory_space=pltpu.VMEM),
        scratch_shapes=[
            pltpu.VMEM((sa, ta, 2, rows, eig), jnp.bfloat16),
            pltpu.VMEM((2, ops_count, eig, eig), jnp.bfloat16),
            pltpu.VMEM((sa * CAP, eig, 2 * eig), jnp.bfloat16),
            pltpu.SemaphoreType.DMA((sends,)),
            pltpu.SemaphoreType.DMA((sa, ta)),
            pltpu.SemaphoreType.DMA((2,)),
        ],
        compiler_params=pltpu.CompilerParams(
            collective_id=0, has_side_effects=True, vmem_limit_bytes=56 * 2**20
        ),
        cost_estimate=pl.CostEstimate(
            flops=flops, bytes_accessed=4 * meson_ops.size, transcendentals=0
        ),
    )(op_table, slots, perambulator, meson_ops)
    normalizer = 1.0 / jnp.sqrt(jnp.float32(ids.shape[0] * eig))
    return (result * normalizer)[:, None, None]


def solution(mesh):
    in_specs = (
        P(None, None, "sa", "ta", None),
        P(None, None, "ta", None, None),
        P("ta", "sa", None),
    )
    out_specs = P(None, "ta", "sa", None, None)
    return jax.shard_map(
        functools.partial(body, mesh.shape["ta"], mesh.shape["sa"]),
        mesh=mesh, in_specs=in_specs, out_specs=out_specs, check_vma=False,
    )
```
